512 devices in a mesh: pipe: 16 (over z, x_lo), expert: 32 (over y, x_hi, core).
Axes of the slice: x: 4 (x_hi: 2, x_lo: 2; x = x_hi * 2 + x_lo), y: 8, z: 8, core: 2. Of those that a mesh axis runs over, the one named last changes fastest.
Arguments:
- fwd_tokens: bfloat16 [16, 1024, 7168], P('pipe', 'expert'), may hold values from -6 to 6
- fwd_routes: int32 [16, 4096, 4], P('pipe', 'expert'), may hold values from 0 to 31, all different within a row; in each aligned block of 128 rows (0 to 127, 128 to 255, ..., all dimensions but the last counted through in order) at most 24 rows name the same one
- fwd_mix: float32 [16, 4096, 4], P('pipe', 'expert'), may hold values from 0.2 to 1
- bwd_tokens: bfloat16 [16, 1024, 7168], P('pipe', 'expert'), may hold values from -6 to 6
- bwd_cotangent: bfloat16 [16, 1024, 7168], P('pipe', 'expert'), may hold values from -6 to 6
- bwd_routes: int32 [16, 4096, 4], P('pipe', 'expert'), may hold values from 0 to 31, all different within a row; in each aligned block of 128 rows (0 to 127, 128 to 255, ..., all dimensions but the last counted through in order) at most 24 rows name the same one
- bwd_mix: float32 [16, 4096, 4], P('pipe', 'expert'), may hold values from 0.2 to 1
- gate_up: bfloat16 [16, 32, 1792, 512], P('pipe', 'expert'), may hold values from -0.125 to 0.125
- down: bfloat16 [16, 32, 256, 1792], P('pipe', 'expert'), may hold values from -0.375 to 0.375
Outputs:
- next_forward: bfloat16 [16, 1024, 7168], P('pipe', 'expert')
- next_backward: bfloat16 [16, 1024, 7168], P('pipe', 'expert')
The draws below stay inside these ranges and needn't reach their ends.
Inputs may be any that keep to these rules, and one draw needn't show every extreme that they name: `fwd_routes`: within the rows of one device (aligned blocks of 128 rows of a section) no expert is named by more than 24 rows, and a row names 4 different experts. `bwd_routes`: within the rows of one device (aligned blocks of 128 rows of a section) no expert is named by more than 24 rows, and a row names 4 different experts.
All inputs are finite; a program needn't handle non-finite values.
Results may differ from the reference program's by a relative error of at most 0.0057.
Values may be sent and summed in bfloat16 or wider, within the bound.
A program may use at most 64 MiB of HBM per device.

```python
import math
import jax
import jax.numpy as jnp
import numpy as np
from jax import lax

D = 7168
HEADS = 4
HD = 1792
FFH = 256
TOP = 4
TOK_DEV = 32
EXPERTS = 32
SECTIONS = 16
TOKENS = 1024
SUBS = 4096
CAP = 24
N_EXPERT = 32


def shard_levels(own_key, dims, pieces, least, top_value):
    factor_of, own = 1.0, jax.random.fold_in(own_key, 6)
    for axis_at, shards_of in pieces:
        draws = jnp.exp(jax.random.uniform(jax.random.fold_in(own, axis_at), (shards_of,), jnp.float32, least / len(pieces), top_value / len(pieces)))
        factor_of = factor_of * jnp.repeat(draws, dims[axis_at] // shards_of).reshape([-1 if axis == axis_at else 1 for axis in range(len(dims))])
    return factor_of


def shared_out(own_key, own, number, rows, count, top, most, skew):
    order = jax.random.permutation(own_key, count)
    heavy_load, common = portions_of(count, rows * top, most, skew, True), portions_of(count, rows * top, most, skew, False)
    places = jnp.arange(count)

    def named(tallies, offset_by):
        used = int((tallies > 0).sum())
        fixed = max(1, used // 4)
        shifted = fixed + (places - fixed + offset_by * (used - fixed)) % max(1, count - fixed)
        return jnp.zeros((count,), jnp.int32).at[order[jnp.where(places < fixed, places, shifted)]].set(jnp.asarray(tallies, jnp.int32))

    tallies = jnp.where(number % 4 == 0, named(heavy_load, number // 4), named(common, number - number // 4 - 1))
    mixed = jax.random.permutation(jax.random.fold_in(own, 3), count)
    source_of, receiver = mixed[0:count // 2 * 2:2], mixed[1:count // 2 * 2:2]
    margin = jnp.minimum(tallies[source_of] - 1, most - tallies[receiver]) // 2
    margin = jnp.where((source_of == order[0]) | (receiver == order[0]) | (tallies[receiver] == 0), 0, jnp.maximum(margin, 0))
    shifted = jax.random.randint(jax.random.fold_in(own, 4), (count // 2,), 0, 1 << 20) % (margin + 1)
    tallies = tallies.at[source_of].add(-shifted).at[receiver].add(shifted)
    members = jnp.searchsorted(jnp.cumsum(tallies), jnp.arange(rows * top), side="right").astype(jnp.int32)
    grid = members.reshape(top, rows).T
    grid = grid[jax.random.permutation(jax.random.fold_in(own, 1), rows)]
    offset_by = jax.random.randint(jax.random.fold_in(own, 2), (rows, 1), 0, top)
    return jnp.take_along_axis(grid, (jnp.arange(top)[None, :] + offset_by) % top, axis=1)


def portions_of(amount, total, limit, skew, full):
    portions = [(1 << 20) // math.isqrt(rank ** skew) + 1 for rank in range(1, amount + 1)]
    largest = limit if full else min(limit, max(-(-total // amount), total * portions[0] // sum(portions)))
    least = 1 if total - largest >= amount - 1 else 0
    given, surplus = [largest] + [least] * (amount - 1), total - largest - least * (amount - 1)
    while surplus > 0:
        candidates = [i for i in range(1, amount) if given[i] < largest] or [i for i in range(1, amount) if given[i] < limit]
        pool, budget = sum([portions[i] for i in candidates]), surplus
        for i in candidates:
            more = min(limit - given[i], max(1, budget * portions[i] // pool), surplus)
            given[i] = given[i] + more
            surplus = surplus - more
    return np.array(given)


def scatter_about(key, dims, spread, limit, pieces=(), held_as=jnp.bfloat16):
    gain = shard_levels(key, dims, pieces, -0.22, 0.18) if pieces else 1.0
    drawn = jax.random.normal(key, dims, jnp.float32) * spread * gain
    return jnp.minimum(jnp.maximum(drawn, -limit), limit).astype(held_as)


def setup_inputs(seed: int = 0) -> dict:
    splits = jax.random.split(jax.random.key(seed), 10)
    fwd_tokens = scatter_about(splits[0], (SECTIONS, TOKENS, D), 1.0, 6.0, ((0, 16), (1, 32)))
    fwd_routes_keys = jax.random.split(jax.random.fold_in(splits[1], 1), SECTIONS * SUBS // (TOK_DEV * HEADS))
    fwd_routes_turns = jax.random.permutation(jax.random.fold_in(splits[1], 3), SECTIONS * SUBS // (TOK_DEV * HEADS))
    fwd_routes = jax.vmap(lambda own, number: shared_out(jax.random.fold_in(splits[1], 2), own, number, TOK_DEV * HEADS, EXPERTS, TOP, CAP, 2))(fwd_routes_keys, fwd_routes_turns).reshape((SECTIONS, SUBS, TOP))
    fwd_mix = jnp.clip(0.2 + 0.8 * jax.random.uniform(splits[2], (SECTIONS, SUBS, TOP), jnp.float32) ** shard_levels(splits[2], (SECTIONS, SUBS, TOP), ((0, 16), (1, 32)), -0.2, 0.2), 0.2, 1.0)
    bwd_tokens = scatter_about(splits[3], (SECTIONS, TOKENS, D), 1.0, 6.0, ((0, 16), (1, 32)))
    bwd_cotangent = scatter_about(splits[4], (SECTIONS, TOKENS, D), 1.0, 6.0, ((0, 16), (1, 32)))
    bwd_routes_keys = jax.random.split(jax.random.fold_in(splits[5], 1), SECTIONS * SUBS // (TOK_DEV * HEADS))
    bwd_routes_turns = jax.random.permutation(jax.random.fold_in(splits[5], 3), SECTIONS * SUBS // (TOK_DEV * HEADS))
    bwd_routes = jax.vmap(lambda own, number: shared_out(jax.random.fold_in(splits[5], 2), own, number, TOK_DEV * HEADS, EXPERTS, TOP, CAP, 2))(bwd_routes_keys, bwd_routes_turns).reshape((SECTIONS, SUBS, TOP))
    bwd_mix = jnp.clip(0.2 + 0.8 * jax.random.uniform(splits[6], (SECTIONS, SUBS, TOP), jnp.float32) ** shard_levels(splits[6], (SECTIONS, SUBS, TOP), ((0, 16), (1, 32)), -0.2, 0.2), 0.2, 1.0)
    gate_up = scatter_about(splits[7], (SECTIONS, EXPERTS, HD, 2 * FFH), HD ** -0.5, 0.125, ((0, 16), (1, 32)))
    down = scatter_about(splits[8], (SECTIONS, EXPERTS, FFH, HD), FFH ** -0.5, 0.375, ((0, 16), (1, 32)))
    return {"fwd_tokens": fwd_tokens, "fwd_routes": fwd_routes, "fwd_mix": fwd_mix, "bwd_tokens": bwd_tokens, "bwd_cotangent": bwd_cotangent, "bwd_routes": bwd_routes, "bwd_mix": bwd_mix, "gate_up": gate_up, "down": down}


def block_places(routes, capacity, count_experts):
    flat_routes = routes.reshape(-1)
    onehot = (flat_routes[:, None] == jnp.arange(count_experts, dtype=jnp.int32)[None, :]).astype(jnp.int32)
    before = jnp.cumsum(onehot, axis=0) - onehot
    slot_index = jnp.sum(before * onehot, axis=1)
    return flat_routes, slot_index


def expert_forward(send_rows, w_gate_up, w_down):
    token_rows = send_rows.reshape(-1, send_rows.shape[-1])
    projected = jnp.dot(token_rows, w_gate_up, preferred_element_type=jnp.float32)
    width_hidden = w_down.shape[0]
    gate_value = projected[:, :width_hidden]
    up_value = projected[:, width_hidden:]
    hidden = (jax.nn.silu(gate_value) * up_value).astype(jnp.bfloat16)
    expert_out = jnp.dot(hidden, w_down, preferred_element_type=jnp.float32).astype(jnp.bfloat16)
    return expert_out.reshape(send_rows.shape)


def expert_backward(input_rows, grad_rows, w_gate_up, w_down):
    token_rows = input_rows.reshape(-1, input_rows.shape[-1])
    cotan_rows = grad_rows.reshape(-1, grad_rows.shape[-1])
    projected = jnp.dot(token_rows, w_gate_up, preferred_element_type=jnp.float32)
    width_hidden = w_down.shape[0]
    gate_value = projected[:, :width_hidden]
    up_value = projected[:, width_hidden:]
    sigmoid_gate = jax.nn.sigmoid(gate_value)
    d_hidden = jnp.dot(cotan_rows, w_down.T, preferred_element_type=jnp.float32)
    d_gate = d_hidden * up_value * sigmoid_gate * (1.0 + gate_value * (1.0 - sigmoid_gate))
    d_up = d_hidden * gate_value * sigmoid_gate
    d_both = jnp.concatenate([d_gate, d_up], axis=1).astype(jnp.bfloat16)
    d_rows = jnp.dot(d_both, w_gate_up.T, preferred_element_type=jnp.float32).astype(jnp.bfloat16)
    return d_rows.reshape(input_rows.shape)


def section_targets(routes):
    blocks = routes.reshape(N_EXPERT, TOK_DEV * HEADS, TOP)
    experts_of, slots_of = jax.vmap(lambda blk: block_places(blk, CAP, EXPERTS))(blocks)
    block_ids = jnp.arange(N_EXPERT, dtype=jnp.int32)[:, None]
    target_rows = experts_of * (N_EXPERT * CAP) + block_ids * CAP + slots_of
    return target_rows.reshape(-1)


def scatter_rows(source, target_rows):
    repeated = jnp.repeat(source.reshape(SUBS, HD), TOP, axis=0)
    send_rows = jnp.zeros((EXPERTS * N_EXPERT * CAP, HD), jnp.bfloat16).at[target_rows].set(repeated)
    return send_rows.reshape(EXPERTS, N_EXPERT * CAP, HD)


def combine(returned, target_rows, mix_weights):
    picked = returned.reshape(-1, HD)[target_rows].astype(jnp.float32).reshape(SUBS, TOP, HD)
    mixed = jnp.sum(mix_weights[:, :, None] * picked, axis=1)
    return mixed.astype(jnp.bfloat16).reshape(TOKENS, D)


def one_section(operands):
    fwd_tok, fwd_rt, fwd_mx, bwd_tok, bwd_cot, bwd_rt, bwd_mx, w_gate_up, w_down = operands
    target_fwd = section_targets(fwd_rt)
    target_bwd = section_targets(bwd_rt)
    send_fwd = scatter_rows(fwd_tok, target_fwd)
    send_inp = scatter_rows(bwd_tok, target_bwd)
    send_cot = scatter_rows(bwd_cot, target_bwd)
    out_fwd = lax.map(lambda ops: expert_forward(ops[0], ops[1], ops[2]), (send_fwd, w_gate_up, w_down))
    out_bwd = lax.map(lambda ops: expert_backward(ops[0], ops[1], ops[2], ops[3]), (send_inp, send_cot, w_gate_up, w_down))
    forward_out = combine(out_fwd, target_fwd, fwd_mx)
    backward_out = combine(out_bwd, target_bwd, bwd_mx)
    return forward_out, backward_out


def reference(fwd_tokens, fwd_routes, fwd_mix, bwd_tokens, bwd_cotangent, bwd_routes, bwd_mix, gate_up, down):
    forward_out, backward_out = lax.map(one_section, (fwd_tokens, fwd_routes, fwd_mix, bwd_tokens, bwd_cotangent, bwd_routes, bwd_mix, gate_up, down))
    return jnp.roll(forward_out, 1, axis=0), jnp.roll(backward_out, -1, axis=0)
```

```python
import functools

import jax
import jax.numpy as jnp
from jax import lax
from jax.experimental import pallas as pl
from jax.experimental.pallas import tpu as pltpu
from jax.sharding import PartitionSpec as P

MESH = pl.DeviceIdType.MESH
RING = 8
PLANE = 4
TOP = 4
ROWS = 128
HALF = ROWS // 2
PART = 32
WIDTH = 1792
HID = 256
PIECES = 6
FWD, SAVED, COT = 0, 1, 2
PLUS, MINUS = 0, 1

OWN, FAR = 0, 1


def place(distance, way):
    return 2 * distance + way


STEP_ROW = {1: 0, 2: HALF, 3: HALF + ROWS, 4: HALF + 2 * ROWS}


def dot(a, b):
    return jnp.dot(a, b, preferred_element_type=jnp.float32)


def dot_t(a, b):
    return lax.dot_general(a, b, (((1,), (1,)), ((), ())), preferred_element_type=jnp.float32)


def kernel(
    fwd_tokens, fwd_routes, fwd_mix, saved, cotangent, bwd_routes, bwd_mix, gate_up, down,
    out_fwd, out_bwd,
    x, gu, dn, part, got, begun, done, hid, both, wt, wr, wc,
    load_sem, gs, gr, ss, sr, os_, or_, xs, xr, cs, cr, rs, rr, ws, wrs,
):
    ex = lax.axis_index("expert")
    pi = lax.axis_index("pipe")
    sections = 16
    y = ex // PLANE
    seat = ex % PLANE
    xh = seat // 2
    core = seat % 2

    def ring(delta):
        return {"pipe": pi, "expert": ((y + delta) % RING) * PLANE + seat}

    mate_seat = (1 - xh) * 2 + core
    mate = {"pipe": pi, "expert": y * PLANE + mate_seat}
    twin = {"pipe": pi, "expert": y * PLANE + xh * 2 + (1 - core)}
    later = {"pipe": (pi + 1) % sections, "expert": ex}
    earlier = {"pipe": (pi + sections - 1) % sections, "expert": ex}
    side = {PLUS: ring(1), MINUS: ring(RING - 1)}

    def load(index, source, target):
        copy = pltpu.make_async_copy(source, target, load_sem.at[index])
        copy.start()
        return copy

    token_loads = []
    for a, source in enumerate((fwd_tokens, saved, cotangent)):
        token_loads.append([
            load(4 * a + h, source.at[0, :, pl.ds(h * WIDTH, WIDTH)], x.at[a, pl.ds(PART * h, PART), :])
            for h in range(4)
        ])
    weight_loads = [load(12, gate_up.at[0, 0], gu.at[seat]), load(13, down.at[0, 0], dn.at[seat])]

    barrier = pltpu.get_barrier_semaphore()
    met = [ring(d) for d in range(1, RING)] + [mate, twin, later, earlier]
    for device in met:
        pl.semaphore_signal(barrier, inc=1, device_id=device, device_id_type=MESH)
    pl.semaphore_wait(barrier, len(met))

    def remote(source, target, send, receive, device):
        return pltpu.make_async_remote_copy(
            src_ref=source, dst_ref=target, send_sem=send, recv_sem=receive,
            device_id=device, device_id_type=MESH,
        )

    def gather(a, way, hop):
        index = (a * 2 + way) * 4 + hop - 1
        if hop == 4:
            low = HALF * way
            source = x.at[a, pl.ds(place(3, way) * ROWS + low, HALF), :]
            target = x.at[a, pl.ds(FAR * ROWS + low, HALF), :]
        else:
            source = x.at[a, pl.ds((place(hop - 1, way) if hop > 1 else OWN) * ROWS, ROWS), :]
            target = x.at[a, pl.ds(place(hop, way) * ROWS, ROWS), :]
        return remote(source, target, gs.at[index], gr.at[index], side[way])

    def gather_start(a, hop):
        for way in (PLUS, MINUS):
            gather(a, way, hop).start()

    def gather_wait(a, hop):
        for way in (PLUS, MINUS):
            gather(a, way, hop).wait_recv()

    def relay(a, hop):
        gather_wait(a, hop)
        gather_start(a, hop + 1)

    for a in (FWD, SAVED, COT):
        for copy in token_loads[a]:
            copy.wait()
        gather_start(a, 1)

    def piece(owner, i):
        if i < 4:
            return gu.at[owner, pl.ds(448 * i, 448), :]
        return dn.at[owner, pl.ds(128 * (i - 4), 128), :]

    for copy in weight_loads:
        copy.wait()
    to_mate = [remote(piece(seat, i), piece(seat, i), xs.at[i], xr.at[i], mate) for i in range(PIECES)]
    to_twin = [remote(piece(seat, i), piece(seat, i), cs.at[i], cr.at[i], twin) for i in range(PIECES)]
    passed = [
        remote(piece(mate_seat, i), piece(mate_seat, i), rs.at[i], rr.at[i], twin) for i in range(PIECES)
    ]
    for i in range(PIECES):
        to_mate[i].start()
    for i in range(PIECES):
        to_twin[i].start()

    lane = lax.broadcasted_iota(jnp.int32, (ROWS, ROWS), 1)
    row = lax.broadcasted_iota(jnp.int32, (ROWS, ROWS), 0)
    order = (row == (lane % PART) * 4 + lane // PART).astype(jnp.float32)

    def by_expert(routes, mix):
        chosen = routes[0]
        weight = mix[0]
        spread = jnp.zeros((ROWS, ROWS), jnp.float32)
        for k in range(TOP):
            spread = spread + jnp.where(chosen[:, k : k + 1] == lane, weight[:, k : k + 1], 0.0)
        return jnp.dot(spread.T, order, precision=lax.Precision.HIGHEST, preferred_element_type=jnp.float32)

    for a, (routes, mix) in enumerate(((fwd_routes, fwd_mix), (bwd_routes, bwd_mix))):
        table = by_expert(routes, mix)
        for at in range(RING):
            wt[at, pl.ds(4 * a, 4), :] = table[4 * at : 4 * at + 4, :]

    def source_place(delta):
        if delta == 4:
            return FAR
        return place(delta, PLUS) if delta < 4 else place(RING - delta, MINUS)

    mixes = [
        remote(wt.at[(y + d) % RING], wr.at[source_place(d)], ws.at[d - 1], wrs.at[d - 1], ring(d))
        for d in range(1, RING)
    ]
    for copy in mixes:
        copy.start()
    wr[OWN] = wt[y]

    relay(FWD, 1)
    relay(SAVED, 1)
    relay(COT, 1)
    for copy in mixes:
        copy.wait_recv()
    for s in range(RING):
        wc[pl.ds(s * ROWS, ROWS), :] = wr[s].T
    relay(FWD, 2)
    relay(SAVED, 2)
    relay(COT, 2)
    for i in range(PIECES):
        to_mate[i].wait_recv()
        passed[i].start()
    for i in range(PIECES):
        to_twin[i].wait_recv()
    for i in range(PIECES):
        passed[i].wait_recv()

    def compute_fwd(pair):
        rows = pl.ds(pair * 2 * ROWS, 2 * ROWS)
        for e in range(PLANE):
            projected = dot(x[FWD, rows, :], gu[e])
            gate, up = projected[:, :HID], projected[:, HID:]
            hidden = gate * jax.nn.sigmoid(gate) * up * wc[rows, e : e + 1]
            hid[:, e * HID : (e + 1) * HID] = hidden.astype(jnp.bfloat16)
        for n in range(WIDTH // 256):
            cols = slice(n * 256, (n + 1) * 256)
            total = dot(hid[:, :HID], dn[0, :, cols])
            for e in range(1, PLANE):
                total = total + dot(hid[:, e * HID : (e + 1) * HID], dn[e, :, cols])
            part[0, rows, cols] = total

    def compute_bwd(pair):
        rows = pl.ds(pair * 2 * ROWS, 2 * ROWS)
        for e in range(PLANE):
            projected = dot(x[SAVED, rows, :], gu[e])
            gate, up = projected[:, :HID], projected[:, HID:]
            d_hidden = dot_t(x[COT, rows, :], dn[e]) * wc[rows, 4 + e : 5 + e]
            sig = jax.nn.sigmoid(gate)
            d_gate = d_hidden * up * sig * (1.0 + gate * (1.0 - sig))
            d_up = d_hidden * gate * sig
            both[:, e * 2 * HID : e * 2 * HID + HID] = d_gate.astype(jnp.bfloat16)
            both[:, e * 2 * HID + HID : (e + 1) * 2 * HID] = d_up.astype(jnp.bfloat16)
        for n in range(WIDTH // 256):
            cols = slice(n * 256, (n + 1) * 256)
            total = dot_t(both[:, : 2 * HID], gu[0, cols, :])
            for e in range(1, PLANE):
                total = total + dot_t(both[:, e * 2 * HID : (e + 1) * 2 * HID], gu[e, cols, :])
            part[1, rows, cols] = total

    def back_copy(m, way, step, h):
        index = ((m * 2 + way) * 4 + step - 1) * 4 + h
        here = HALF if step == 1 else ROWS
        low = PART * h - (HALF * way if step == 1 else 0)
        fresh = step == 1 or (step == 2 and h // 2 != way)
        if fresh:
            at = (0 if step == 1 else HALF) + PART * (h % 2)
            source = begun.at[m, way, pl.ds(at, PART), :]
        else:
            before = PART * h - (HALF * way if step == 2 else 0)
            source = got.at[m, way, pl.ds(STEP_ROW[step - 1] + before, PART), :]
        target = got.at[m, way, pl.ds(STEP_ROW[step] + low, PART), :]
        return remote(source, target, ss.at[index], sr.at[index], side[1 - way])

    def block_at(step, way):
        return FAR if step == 1 else place(5 - step, way)

    def back_fresh(m, way, step, h):
        at = (0 if step == 1 else HALF) + PART * (h % 2)
        begun[m, way, pl.ds(at, PART), :] = part[
            m, pl.ds(block_at(step, way) * ROWS + PART * h, PART), :
        ].astype(jnp.bfloat16)
        back_copy(m, way, step, h).start()

    def back_begin(m):
        for h in range(2):
            for way in (PLUS, MINUS):
                back_fresh(m, way, 1, h + 2 * way)

    def back_begin_second(m):
        for h in range(2):
            for way in (PLUS, MINUS):
                back_fresh(m, way, 2, h + 2 * (1 - way))

    def back_add(m, way, step, h):
        back_copy(m, way, step - 1, h).wait_recv()
        before = PART * h - (HALF * way if step == 2 else 0)
        rows = pl.ds(STEP_ROW[step - 1] + before, PART)
        mine = part[m, pl.ds(block_at(step, way) * ROWS + PART * h, PART), :]
        got[m, way, rows, :] = (got[m, way, rows, :].astype(jnp.float32) + mine).astype(jnp.bfloat16)
        back_copy(m, way, step, h).start()

    def back_step(m, step):
        for h in range(2 if step == 2 else 4):
            for way in (PLUS, MINUS):
                if step == 2:
                    back_add(m, way, step, h + 2 * way)
                elif step == 3:
                    back_add(m, way, step, (h + 2 * (1 - way)) % 4)
                else:
                    back_add(m, way, step, (h + 2 * (1 - way)) % 4)

    outs = [
        [
            remote(
                done.at[m, pl.ds(PART * h, PART), :],
                (out_fwd, out_bwd)[m].at[0, :, pl.ds(h * WIDTH, WIDTH)],
                os_.at[m * 4 + h], or_.at[m * 4 + h], (later, earlier)[m],
            )
            for h in range(4)
        ]
        for m in range(2)
    ]

    def finish(m):
        for h in range(4):
            for way in (PLUS, MINUS):
                back_copy(m, way, 4, h).wait_recv()
            rows = pl.ds(PART * h, PART)
            last = pl.ds(STEP_ROW[4] + PART * h, PART)
            total = part[m, pl.ds(OWN * ROWS + PART * h, PART), :]
            for way in (PLUS, MINUS):
                total = total + got[m, way, last, :].astype(jnp.float32)
            done[m, rows, :] = total.astype(jnp.bfloat16)
            outs[m][h].start()

    compute_fwd(1)
    relay(FWD, 3)
    compute_fwd(2)
    relay(SAVED, 3)
    compute_fwd(3)
    compute_bwd(1)
    relay(COT, 3)
    gather_wait(FWD, 4)
    compute_fwd(0)
    back_begin(0)
    back_begin_second(0)
    compute_bwd(2)
    back_step(0, 2)
    compute_bwd(3)
    back_step(0, 3)
    gather_wait(SAVED, 4)
    gather_wait(COT, 4)
    compute_bwd(0)
    back_begin(1)
    back_begin_second(1)
    back_step(0, 4)
    back_step(1, 2)
    finish(0)
    back_step(1, 3)
    back_step(1, 4)
    finish(1)

    for a in (FWD, SAVED, COT):
        for hop in range(1, 5):
            for way in (PLUS, MINUS):
                gather(a, way, hop).wait_send()
    for i in range(PIECES):
        to_mate[i].wait_send()
        to_twin[i].wait_send()
        passed[i].wait_send()
    for copy in mixes:
        copy.wait_send()
    for m in range(2):
        for way in (PLUS, MINUS):
            for step in range(1, 5):
                for h in range(2) if step == 1 else range(4):
                    back_copy(m, way, step, h + 2 * way if step == 1 else h).wait_send()
        for h in range(4):
            outs[m][h].wait_send()
            outs[m][h].wait_recv()


def body(*operands):
    hbm = pl.BlockSpec(memory_space=pl.ANY)
    vmem = pl.BlockSpec(memory_space=pltpu.VMEM)
    out = jax.ShapeDtypeStruct(operands[0].shape, jnp.bfloat16)
    dma = pltpu.SemaphoreType.DMA
    bf16, f32 = jnp.bfloat16, jnp.float32
    return pl.pallas_call(
        kernel,
        out_shape=(out, out),
        in_specs=[hbm, vmem, vmem, hbm, hbm, vmem, vmem, hbm, hbm],
        out_specs=(hbm, hbm),
        scratch_shapes=[
            pltpu.VMEM((3, RING * ROWS, WIDTH), bf16),
            pltpu.VMEM((PLANE, WIDTH, 2 * HID), bf16),
            pltpu.VMEM((PLANE, HID, WIDTH), bf16),
            pltpu.VMEM((2, RING * ROWS, WIDTH), f32),
            pltpu.VMEM((2, 2, HALF + 3 * ROWS, WIDTH), bf16),
            pltpu.VMEM((2, 2, ROWS, WIDTH), bf16),
            pltpu.VMEM((2, ROWS, WIDTH), bf16),
            pltpu.VMEM((2 * ROWS, PLANE * HID), bf16),
            pltpu.VMEM((2 * ROWS, PLANE * 2 * HID), bf16),
            pltpu.VMEM((RING, 8, ROWS), f32),
            pltpu.VMEM((RING, 8, ROWS), f32),
            pltpu.VMEM((RING * ROWS, 8), f32),
            dma((14,)),
            dma((24,)), dma((24,)),
            dma((64,)), dma((64,)),
            dma((8,)), dma((8,)),
            dma((PIECES,)), dma((PIECES,)),
            dma((PIECES,)), dma((PIECES,)),
            dma((PIECES,)), dma((PIECES,)),
            dma((RING - 1,)), dma((RING - 1,)),
        ],
        name="moe_relay",
        compiler_params=pltpu.CompilerParams(
            collective_id=0, has_side_effects=True, vmem_limit_bytes=60 * 1024 * 1024
        ),
    )(*operands)


def solution(mesh):
    spec3 = P("pipe", "expert", None)
    spec4 = P("pipe", "expert", None, None)
    return jax.shard_map(
        body,
        mesh=mesh,
        in_specs=(spec3,) * 7 + (spec4,) * 2,
        out_specs=(spec3, spec3),
        check_vma=False,
    )
```

```python
import functools

import jax
import jax.numpy as jnp
from jax import lax
from jax.experimental import pallas as pl
from jax.experimental.pallas import tpu as pltpu
from jax.sharding import PartitionSpec as P

MESH = pl.DeviceIdType.MESH
RING = 8
PLANE = 4
TOP = 4
ROWS = 128
PART = 32
HOP_ROWS = {1: 128, 2: 128, 3: 112, 4: 48}
LIMIT3, LIMIT4 = float(HOP_ROWS[3]), float(HOP_ROWS[4])
WIDTH = 1792
HID = 256
PIECES = 6
FWD, SAVED, COT = 0, 1, 2
PLUS, MINUS = 0, 1

OWN, FAR = 0, 1


def place(distance, way):
    return 2 * distance + way


BACK_ROWS = {1: 48, 2: 112, 3: 128, 4: 128}
STEP_ROW = {1: 0, 2: 112, 3: 240, 4: 368}
GOT_ROWS = 496
COLS = [(0, 512), (512, 512), (1024, 384), (1408, 384)]


def dot(a, b):
    return jnp.dot(a, b, preferred_element_type=jnp.float32)


def dot_t(a, b):
    return lax.dot_general(a, b, (((1,), (1,)), ((), ())), preferred_element_type=jnp.float32)


def kernel(
    fwd_tokens, fwd_routes, fwd_mix, saved, cotangent, bwd_routes, bwd_mix, gate_up, down,
    out_fwd, out_bwd,
    x, xp, gu, dn, part, got, begun, done, hid, both, perm, back, wt, wr, wc,
    load_sem, gs, gr, ss, sr, os_, or_, xs, xr, cs, cr, rs, rr, ws, wrs,
):
    ex = lax.axis_index("expert")
    pi = lax.axis_index("pipe")
    sections = 16
    y = ex // PLANE
    seat = ex % PLANE
    xh = seat // 2
    core = seat % 2

    def ring(delta):
        return {"pipe": pi, "expert": ((y + delta) % RING) * PLANE + seat}

    mate_seat = (1 - xh) * 2 + core
    mate = {"pipe": pi, "expert": y * PLANE + mate_seat}
    twin = {"pipe": pi, "expert": y * PLANE + xh * 2 + (1 - core)}
    later = {"pipe": (pi + 1) % sections, "expert": ex}
    earlier = {"pipe": (pi + sections - 1) % sections, "expert": ex}
    side = {PLUS: ring(1), MINUS: ring(RING - 1)}

    def load(index, source, target):
        copy = pltpu.make_async_copy(source, target, load_sem.at[index])
        copy.start()
        return copy

    token_loads = []
    for a, source in enumerate((fwd_tokens, saved, cotangent)):
        token_loads.append([
            load(4 * a + h, source.at[0, :, pl.ds(h * WIDTH, WIDTH)], x.at[a, pl.ds(PART * h, PART), :])
            for h in range(4)
        ])
    weight_loads = [load(12, gate_up.at[0, 0], gu.at[seat]), load(13, down.at[0, 0], dn.at[seat])]

    barrier = pltpu.get_barrier_semaphore()
    met = [ring(d) for d in range(1, RING)] + [mate, twin, later, earlier]
    for device in met:
        pl.semaphore_signal(barrier, inc=1, device_id=device, device_id_type=MESH)

    lane = lax.broadcasted_iota(jnp.int32, (ROWS, ROWS), 1)
    row = lax.broadcasted_iota(jnp.int32, (ROWS, ROWS), 0)
    order = (row == (lane % PART) * 4 + lane // PART).astype(jnp.float32)
    before = (row < lane).astype(jnp.float32)
    row8 = lax.broadcasted_iota(jnp.int32, (8, ROWS), 0)

    def stack(values):
        total = jnp.zeros((8, ROWS), jnp.float32)
        for i, value in enumerate(values):
            total = total + jnp.where(row8 == i, value, 0.0)
        return total

    def ranked(values):
        stacked = stack(values)
        ranks = dot(stacked, before)
        counts = jnp.sum(stacked, axis=1, keepdims=True)
        n = len(values)
        return [ranks[i : i + 1] for i in range(n)], [counts[i : i + 1] for i in range(n)]

    def make_orders(m, routes):
        away = (routes[0] // PLANE - y + RING) % RING
        flags = [
            jnp.sum((away == d).astype(jnp.float32), axis=0, keepdims=True) for d in (3, 4, 5)
        ]
        flags = jnp.minimum(dot(stack(flags), order), 1.0)
        p3, f4, m3 = flags[0:1], flags[1:2], flags[2:3]
        fa, fb = f4 * p3 * m3, f4 * p3 * (1.0 - m3)
        fc, fd = f4 * (1.0 - p3) * m3, f4 * (1.0 - p3) * (1.0 - m3)
        (ra, rb, rc, rd, _, _), (na, nb, nc, nd, n3p, n3m) = ranked([fa, fb, fc, fd, p3, m3])
        b_in, c_out = jnp.minimum(nb, LIMIT4), jnp.minimum(nc, LIMIT4)
        b_out, c_in = nb - b_in, nc - c_out
        d_in = jnp.maximum(nd - jnp.minimum(LIMIT3 - n3m - b_out, LIMIT4 - c_out - b_out), 0.0)
        a_in = jnp.minimum(na, LIMIT4 - b_in - c_in - d_in)
        plus4 = (
            jnp.where(ra < a_in, fa, 0.0) + jnp.where(rb < b_in, fb, 0.0)
            + jnp.where(rc < c_out, 0.0, fc) + jnp.where(rd < d_in, fd, 0.0)
        )
        minus4 = f4 - plus4
        plus3, minus3 = p3 * (1.0 - plus4), m3 * (1.0 - minus4)
        groups = [plus4, plus3, 1.0 - plus4 - plus3, minus4, minus3, 1.0 - minus4 - minus3]
        ranks, counts = ranked(groups)
        for way in (PLUS, MINUS):
            g, r, n = (v[3 * way : 3 * way + 3] for v in (groups, ranks, counts))
            spot = g[0] * r[0] + g[1] * (n[0] + r[1]) + g[2] * (n[0] + n[1] + r[2])
            perm[m, way] = (row == spot.astype(jnp.int32)).astype(jnp.bfloat16)
        spot = plus4 * ranks[0] + minus4 * (LIMIT4 + ranks[3]) + (1.0 - f4) * 1024.0
        perm[m, 2] = (row == spot.astype(jnp.int32)).astype(jnp.bfloat16)

    def sort_rows(a, m):
        for way in (PLUS, MINUS):
            for start, size in COLS:
                cols = slice(start, start + size)
                xp[a, way, :, cols] = dot(perm[m, way], x[a, :ROWS, cols]).astype(jnp.bfloat16)

    def remote(source, target, send, receive, device):
        return pltpu.make_async_remote_copy(
            src_ref=source, dst_ref=target, send_sem=send, recv_sem=receive,
            device_id=device, device_id_type=MESH,
        )

    def gather(a, way, hop):
        index = (a * 2 + way) * 4 + hop - 1
        count = HOP_ROWS[hop]
        if hop == 1:
            source = xp.at[a, way]
        else:
            source = x.at[a, pl.ds(place(hop - 1, way) * ROWS, count), :]
        start = FAR * ROWS + HOP_ROWS[4] * way if hop == 4 else place(hop, way) * ROWS
        target = x.at[a, pl.ds(start, count), :]
        return remote(source, target, gs.at[index], gr.at[index], side[way])

    def gather_start(a, hop):
        for way in (PLUS, MINUS):
            gather(a, way, hop).start()

    def gather_wait(a, hop):
        for way in (PLUS, MINUS):
            gather(a, way, hop).wait_recv()

    def relay(a, hop):
        gather_wait(a, hop)
        gather_start(a, hop + 1)

    make_orders(0, fwd_routes)
    for copy in token_loads[FWD]:
        copy.wait()
    sort_rows(FWD, 0)
    pl.semaphore_wait(barrier, len(met))
    gather_start(FWD, 1)

    def piece(owner, i):
        if i < 4:
            return gu.at[owner, pl.ds(448 * i, 448), :]
        return dn.at[owner, pl.ds(128 * (i - 4), 128), :]

    for copy in weight_loads:
        copy.wait()
    to_mate = [remote(piece(seat, i), piece(seat, i), xs.at[i], xr.at[i], mate) for i in range(PIECES)]
    to_twin = [remote(piece(seat, i), piece(seat, i), cs.at[i], cr.at[i], twin) for i in range(PIECES)]
    passed = [
        remote(piece(mate_seat, i), piece(mate_seat, i), rs.at[i], rr.at[i], twin) for i in range(PIECES)
    ]
    for i in range(PIECES):
        to_mate[i].start()
    for i in range(PIECES):
        to_twin[i].start()

    make_orders(1, bwd_routes)
    for a in (SAVED, COT):
        for copy in token_loads[a]:
            copy.wait()
        sort_rows(a, 1)
        gather_start(a, 1)

    expert = lax.broadcasted_iota(jnp.int32, (RING * PLANE, ROWS), 0)
    for m, (routes, mix) in enumerate(((fwd_routes, fwd_mix), (bwd_routes, bwd_mix))):
        spread = jnp.zeros((RING * PLANE, ROWS), jnp.float32)
        for k in range(TOP):
            spread = spread + jnp.where(routes[0, k : k + 1, :] == expert, mix[0, k : k + 1, :], 0.0)
        exact = dict(precision=lax.Precision.HIGHEST, preferred_element_type=jnp.float32)
        natural = jnp.dot(spread, order, **exact)
        for kind in range(4):
            if kind < 3:
                moved = perm[m, kind].astype(jnp.float32)
                value = lax.dot_general(natural, moved, (((1,), (1,)), ((), ())), **exact)
            else:
                value = natural
            for at in range(RING):
                wt[kind, at, pl.ds(4 * m, 4), :] = value[4 * at : 4 * at + 4, :]
        for way in (PLUS, MINUS):
            back[m, way] = perm[m, way].astype(jnp.float32).T.astype(jnp.bfloat16)

    def source_place(delta):
        if delta == 4:
            return FAR
        return place(delta, PLUS) if delta < 4 else place(RING - delta, MINUS)

    mixes = [
        remote(wt.at[(0 if d < 4 else 2 if d == 4 else 1), (y + d) % RING], wr.at[source_place(d)], ws.at[d - 1], wrs.at[d - 1], ring(d))
        for d in range(1, RING)
    ]
    for copy in mixes:
        copy.start()
    wr[OWN] = wt[3, y]

    relay(FWD, 1)
    relay(SAVED, 1)
    relay(COT, 1)
    for copy in mixes:
        copy.wait_recv()
    for s in range(RING):
        wc[pl.ds(s * ROWS, ROWS), :] = wr[s].T
    relay(FWD, 2)
    relay(SAVED, 2)
    relay(COT, 2)
    for i in range(PIECES):
        to_mate[i].wait_recv()
        passed[i].start()
    for i in range(PIECES):
        to_twin[i].wait_recv()
    for i in range(PIECES):
        passed[i].wait_recv()

    def compute_fwd(pair):
        rows = pl.ds(pair * 2 * ROWS, 2 * ROWS)
        for e in range(PLANE):
            projected = dot(x[FWD, rows, :], gu[e])
            gate, up = projected[:, :HID], projected[:, HID:]
            hidden = gate * jax.nn.sigmoid(gate) * up * wc[rows, e : e + 1]
            hid[:, e * HID : (e + 1) * HID] = hidden.astype(jnp.bfloat16)
        for n in range(WIDTH // 256):
            cols = slice(n * 256, (n + 1) * 256)
            total = dot(hid[:, :HID], dn[0, :, cols])
            for e in range(1, PLANE):
                total = total + dot(hid[:, e * HID : (e + 1) * HID], dn[e, :, cols])
            part[0, rows, cols] = total

    def compute_bwd(pair):
        rows = pl.ds(pair * 2 * ROWS, 2 * ROWS)
        for e in range(PLANE):
            projected = dot(x[SAVED, rows, :], gu[e])
            gate, up = projected[:, :HID], projected[:, HID:]
            d_hidden = dot_t(x[COT, rows, :], dn[e]) * wc[rows, 4 + e : 5 + e]
            sig = jax.nn.sigmoid(gate)
            d_gate = d_hidden * up * sig * (1.0 + gate * (1.0 - sig))
            d_up = d_hidden * gate * sig
            both[:, e * 2 * HID : e * 2 * HID + HID] = d_gate.astype(jnp.bfloat16)
            both[:, e * 2 * HID + HID : (e + 1) * 2 * HID] = d_up.astype(jnp.bfloat16)
        for n in range(WIDTH // 256):
            cols = slice(n * 256, (n + 1) * 256)
            total = dot_t(both[:, : 2 * HID], gu[0, cols, :])
            for e in range(1, PLANE):
                total = total + dot_t(both[:, e * 2 * HID : (e + 1) * 2 * HID], gu[e, cols, :])
            part[1, rows, cols] = total

    def back_copy(m, way, step, c):
        index = ((m * 2 + way) * 4 + step - 1) * 4 + c
        start, size = COLS[c]
        cols = pl.ds(start, size)
        count = BACK_ROWS[step]
        if step == 1:
            source = begun.at[m, way, :, cols]
        else:
            source = got.at[m, way, pl.ds(STEP_ROW[step - 1], count), cols]
        target = got.at[m, way, pl.ds(STEP_ROW[step], count), cols]
        return remote(source, target, ss.at[index], sr.at[index], side[1 - way])

    def back_begin(m):
        for c, (start, size) in enumerate(COLS):
            cols = slice(start, start + size)
            for way in (PLUS, MINUS):
                rows = pl.ds(FAR * ROWS + HOP_ROWS[4] * way, HOP_ROWS[4])
                begun[m, way, :, cols] = part[m, rows, cols].astype(jnp.bfloat16)
                back_copy(m, way, 1, c).start()

    def back_step(m, step):
        came, count = BACK_ROWS[step - 1], BACK_ROWS[step]
        for c, (start, size) in enumerate(COLS):
            cols = slice(start, start + size)
            for way in (PLUS, MINUS):
                block = place(5 - step, way) * ROWS
                back_copy(m, way, step - 1, c).wait_recv()
                rows = pl.ds(STEP_ROW[step - 1], came)
                total = got[m, way, rows, cols].astype(jnp.float32) + part[m, pl.ds(block, came), cols]
                got[m, way, rows, cols] = total.astype(jnp.bfloat16)
                if count > came:
                    rest = pl.ds(STEP_ROW[step - 1] + came, count - came)
                    mine = part[m, pl.ds(block + came, count - came), cols]
                    got[m, way, rest, cols] = mine.astype(jnp.bfloat16)
                back_copy(m, way, step, c).start()

    def out_copy(m, c, h):
        start, size = COLS[c]
        index = (m * 4 + c) * 4 + h
        return remote(
            done.at[m, pl.ds(PART * h, PART), pl.ds(start, size)],
            (out_fwd, out_bwd)[m].at[0, :, pl.ds(h * WIDTH + start, size)],
            os_.at[index], or_.at[index], (later, earlier)[m],
        )

    def finish(m):
        for c, (start, size) in enumerate(COLS):
            cols = slice(start, start + size)
            total = part[m, pl.ds(OWN * ROWS, ROWS), cols]
            for way in (PLUS, MINUS):
                back_copy(m, way, 4, c).wait_recv()
                total = total + dot(back[m, way], got[m, way, pl.ds(STEP_ROW[4], ROWS), cols])
            done[m, :, cols] = total.astype(jnp.bfloat16)
            for h in range(4):
                out_copy(m, c, h).start()

    compute_fwd(1)
    relay(FWD, 3)
    compute_fwd(2)
    relay(SAVED, 3)
    compute_fwd(3)
    compute_bwd(1)
    relay(COT, 3)
    gather_wait(FWD, 4)
    compute_fwd(0)
    back_begin(0)
    compute_bwd(2)
    back_step(0, 2)
    compute_bwd(3)
    back_step(0, 3)
    gather_wait(SAVED, 4)
    gather_wait(COT, 4)
    compute_bwd(0)
    back_begin(1)
    back_step(0, 4)
    back_step(1, 2)
    finish(0)
    back_step(1, 3)
    back_step(1, 4)
    finish(1)

    for a in (FWD, SAVED, COT):
        for hop in range(1, 5):
            for way in (PLUS, MINUS):
                gather(a, way, hop).wait_send()
    for i in range(PIECES):
        to_mate[i].wait_send()
        to_twin[i].wait_send()
        passed[i].wait_send()
    for copy in mixes:
        copy.wait_send()
    for m in range(2):
        for c in range(4):
            for step in range(1, 5):
                for way in (PLUS, MINUS):
                    back_copy(m, way, step, c).wait_send()
            for h in range(4):
                out_copy(m, c, h).wait_send()
                out_copy(m, c, h).wait_recv()


def deliver(fwd, bwd, out_fwd, out_bwd):
    out_fwd[...] = fwd[...]
    out_bwd[...] = bwd[...]


def body(fwd_tokens, fwd_routes, fwd_mix, saved, cotangent, bwd_routes, bwd_mix, gate_up, down):
    fwd_routes, fwd_mix, bwd_routes, bwd_mix = (
        jnp.swapaxes(v, 1, 2) for v in (fwd_routes, fwd_mix, bwd_routes, bwd_mix)
    )
    operands = (
        fwd_tokens, fwd_routes, fwd_mix, saved, cotangent, bwd_routes, bwd_mix, gate_up, down
    )
    hbm = pl.BlockSpec(memory_space=pl.ANY)
    vmem = pl.BlockSpec(memory_space=pltpu.VMEM)
    out = jax.ShapeDtypeStruct(operands[0].shape, jnp.bfloat16)
    dma = pltpu.SemaphoreType.DMA
    bf16, f32 = jnp.bfloat16, jnp.float32
    moved = pl.pallas_call(
        kernel,
        out_shape=(out, out),
        in_specs=[hbm, vmem, vmem, hbm, hbm, vmem, vmem, hbm, hbm],
        out_specs=(hbm, hbm),
        scratch_shapes=[
            pltpu.VMEM((3, RING * ROWS, WIDTH), bf16),
            pltpu.VMEM((3, 2, ROWS, WIDTH), bf16),
            pltpu.VMEM((PLANE, WIDTH, 2 * HID), bf16),
            pltpu.VMEM((PLANE, HID, WIDTH), bf16),
            pltpu.VMEM((2, RING * ROWS, WIDTH), f32),
            pltpu.VMEM((2, 2, GOT_ROWS, WIDTH), bf16),
            pltpu.VMEM((2, 2, HOP_ROWS[4], WIDTH), bf16),
            pltpu.VMEM((2, ROWS, WIDTH), bf16),
            pltpu.VMEM((2 * ROWS, PLANE * HID), bf16),
            pltpu.VMEM((2 * ROWS, PLANE * 2 * HID), bf16),
            pltpu.VMEM((2, 3, ROWS, ROWS), bf16),
            pltpu.VMEM((2, 2, ROWS, ROWS), bf16),
            pltpu.VMEM((4, RING, 8, ROWS), f32),
            pltpu.VMEM((RING, 8, ROWS), f32),
            pltpu.VMEM((RING * ROWS, 8), f32),
            dma((14,)),
            dma((24,)), dma((24,)),
            dma((64,)), dma((64,)),
            dma((32,)), dma((32,)),
            dma((PIECES,)), dma((PIECES,)),
            dma((PIECES,)), dma((PIECES,)),
            dma((PIECES,)), dma((PIECES,)),
            dma((RING - 1,)), dma((RING - 1,)),
        ],
        name="moe_relay",
        compiler_params=pltpu.CompilerParams(
            collective_id=0, has_side_effects=True, vmem_limit_bytes=60 * 1024 * 1024
        ),
    )(*operands)
    return pl.pallas_call(
        deliver,
        out_shape=(out, out),
        in_specs=[vmem, vmem],
        out_specs=(vmem, vmem),
        name="deliver",
    )(*moved)


def solution(mesh):
    spec3 = P("pipe", "expert", None)
    spec4 = P("pipe", "expert", None, None)
    return jax.shard_map(
        body,
        mesh=mesh,
        in_specs=(spec3,) * 7 + (spec4,) * 2,
        out_specs=(spec3, spec3),
        check_vma=False,
    )
```

```python
import functools

import jax
import jax.numpy as jnp
from jax import lax
from jax.experimental import pallas as pl
from jax.experimental.pallas import tpu as pltpu
from jax.sharding import PartitionSpec as P

MESH = pl.DeviceIdType.MESH
RING = 8
PLANE = 4
TOP = 4
ROWS = 128
PART = 32
HOP_ROWS = {1: 128, 2: 128, 3: 112, 4: 48}
LIMIT3, LIMIT4 = float(HOP_ROWS[3]), float(HOP_ROWS[4])
WIDTH = 1792
HID = 256
PIECES = 6
FWD, SAVED, COT = 0, 1, 2
PLUS, MINUS = 0, 1

OWN, FAR = 0, 1


def place(distance, way):
    return 2 * distance + way


BACK_ROWS = {1: 48, 2: 112, 3: 128, 4: 128}
STEP_ROW = {1: 0, 2: 112, 3: 240, 4: 368}
GOT_ROWS = 496
COLS = [(0, 512), (512, 512), (1024, 384), (1408, 384)]


def dot(a, b):
    return jnp.dot(a, b, preferred_element_type=jnp.float32)


def dot_t(a, b):
    return lax.dot_general(a, b, (((1,), (1,)), ((), ())), preferred_element_type=jnp.float32)


def kernel(
    fwd_tokens, fwd_routes, fwd_mix, saved, cotangent, bwd_routes, bwd_mix, gate_up, down,
    out_fwd, out_bwd,
    x, xp, gu, dn, part, got, begun, done, hid, both, perm, back, wt, wr, wc,
    load_sem, gs, gr, ss, sr, os_, or_, xs, xr, cs, cr, rs, rr, ws, wrs, twin_here, pipe_here,
):
    ex = lax.axis_index("expert")
    pi = lax.axis_index("pipe")
    sections = 16
    y = ex // PLANE
    seat = ex % PLANE
    xh = seat // 2
    core = seat % 2

    def ring(delta):
        return {"pipe": pi, "expert": ((y + delta) % RING) * PLANE + seat}

    mate_seat = (1 - xh) * 2 + core
    mate = {"pipe": pi, "expert": y * PLANE + mate_seat}
    twin = {"pipe": pi, "expert": y * PLANE + xh * 2 + (1 - core)}
    later = {"pipe": (pi + 1) % sections, "expert": ex}
    earlier = {"pipe": (pi + sections - 1) % sections, "expert": ex}
    side = {PLUS: ring(1), MINUS: ring(RING - 1)}

    barrier = pltpu.get_barrier_semaphore()
    odd = pi % 2
    met = [ring(d) for d in range(1, RING)] + [mate]
    for device in met:
        pl.semaphore_signal(barrier, inc=1, device_id=device, device_id_type=MESH)

    @pl.when(core == 1)
    def _():
        pl.semaphore_signal(barrier, inc=1, device_id=twin, device_id_type=MESH)

    @pl.when(odd == 0)
    def _():
        pl.semaphore_signal(barrier, inc=1, device_id=later, device_id_type=MESH)
        pl.semaphore_signal(barrier, inc=1, device_id=earlier, device_id_type=MESH)

    def load(index, source, target):
        copy = pltpu.make_async_copy(source, target, load_sem.at[index])
        copy.start()
        return copy

    token_loads = []
    for a, source in enumerate((fwd_tokens, saved, cotangent)):
        token_loads.append([
            load(4 * a + h, source.at[0, :, pl.ds(h * WIDTH, WIDTH)], x.at[a, pl.ds(PART * h, PART), :])
            for h in range(4)
        ])
    weight_loads = [load(12, gate_up.at[0, 0], gu.at[seat]), load(13, down.at[0, 0], dn.at[seat])]

    lane = lax.broadcasted_iota(jnp.int32, (ROWS, ROWS), 1)
    row = lax.broadcasted_iota(jnp.int32, (ROWS, ROWS), 0)
    order = (row == (lane % PART) * 4 + lane // PART).astype(jnp.float32)
    before = (row < lane).astype(jnp.float32)
    row8 = lax.broadcasted_iota(jnp.int32, (8, ROWS), 0)

    def stack(values):
        total = jnp.zeros((8, ROWS), jnp.float32)
        for i, value in enumerate(values):
            total = total + jnp.where(row8 == i, value, 0.0)
        return total

    def ranked(values):
        stacked = stack(values)
        ranks = dot(stacked, before)
        counts = jnp.sum(stacked, axis=1, keepdims=True)
        n = len(values)
        return [ranks[i : i + 1] for i in range(n)], [counts[i : i + 1] for i in range(n)]

    def make_orders(m, routes):
        away = (routes[0] // PLANE - y + RING) % RING
        flags = [
            jnp.sum((away == d).astype(jnp.float32), axis=0, keepdims=True) for d in (3, 4, 5)
        ]
        flags = jnp.minimum(dot(stack(flags), order), 1.0)
        p3, f4, m3 = flags[0:1], flags[1:2], flags[2:3]
        fa, fb = f4 * p3 * m3, f4 * p3 * (1.0 - m3)
        fc, fd = f4 * (1.0 - p3) * m3, f4 * (1.0 - p3) * (1.0 - m3)
        (ra, rb, rc, rd, _, _), (na, nb, nc, nd, n3p, n3m) = ranked([fa, fb, fc, fd, p3, m3])
        b_in, c_out = jnp.minimum(nb, LIMIT4), jnp.minimum(nc, LIMIT4)
        b_out, c_in = nb - b_in, nc - c_out
        d_in = jnp.maximum(nd - jnp.minimum(LIMIT3 - n3m - b_out, LIMIT4 - c_out - b_out), 0.0)
        a_in = jnp.minimum(na, LIMIT4 - b_in - c_in - d_in)
        plus4 = (
            jnp.where(ra < a_in, fa, 0.0) + jnp.where(rb < b_in, fb, 0.0)
            + jnp.where(rc < c_out, 0.0, fc) + jnp.where(rd < d_in, fd, 0.0)
        )
        minus4 = f4 - plus4
        plus3, minus3 = p3 * (1.0 - plus4), m3 * (1.0 - minus4)
        groups = [plus4, plus3, 1.0 - plus4 - plus3, minus4, minus3, 1.0 - minus4 - minus3]
        ranks, counts = ranked(groups)
        for way in (PLUS, MINUS):
            g, r, n = (v[3 * way : 3 * way + 3] for v in (groups, ranks, counts))
            spot = g[0] * r[0] + g[1] * (n[0] + r[1]) + g[2] * (n[0] + n[1] + r[2])
            perm[m, way] = (row == spot.astype(jnp.int32)).astype(jnp.bfloat16)
        spot = plus4 * ranks[0] + minus4 * (LIMIT4 + ranks[3]) + (1.0 - f4) * 1024.0
        perm[m, 2] = (row == spot.astype(jnp.int32)).astype(jnp.bfloat16)

    def sort_rows(a, m):
        for way in (PLUS, MINUS):
            for start, size in COLS:
                cols = slice(start, start + size)
                xp[a, way, :, cols] = dot(perm[m, way], x[a, :ROWS, cols]).astype(jnp.bfloat16)

    def remote(source, target, send, receive, device):
        return pltpu.make_async_remote_copy(
            src_ref=source, dst_ref=target, send_sem=send, recv_sem=receive,
            device_id=device, device_id_type=MESH,
        )

    def gather(a, way, hop):
        index = (a * 2 + way) * 4 + hop - 1
        count = HOP_ROWS[hop]
        if hop == 1:
            source = xp.at[a, way]
        else:
            source = x.at[a, pl.ds(place(hop - 1, way) * ROWS, count), :]
        start = FAR * ROWS + HOP_ROWS[4] * way if hop == 4 else place(hop, way) * ROWS
        target = x.at[a, pl.ds(start, count), :]
        return remote(source, target, gs.at[index], gr.at[index], side[way])

    def gather_start(a, hop):
        for way in (PLUS, MINUS):
            gather(a, way, hop).start()

    def gather_wait(a, hop):
        for way in (PLUS, MINUS):
            gather(a, way, hop).wait_recv()

    def relay(a, hop):
        gather_wait(a, hop)
        gather_start(a, hop + 1)

    make_orders(0, fwd_routes)
    for copy in token_loads[FWD]:
        copy.wait()
    sort_rows(FWD, 0)
    pl.semaphore_wait(barrier, len(met) + 1 - core + 2 * odd)

    @pl.when(odd == 1)
    def _():
        pl.semaphore_signal(pipe_here, inc=1, device_id=later, device_id_type=MESH)
        pl.semaphore_signal(pipe_here, inc=1, device_id=earlier, device_id_type=MESH)

    @pl.when(core == 0)
    def _():
        pl.semaphore_signal(twin_here, inc=1, device_id=twin, device_id_type=MESH)

    gather_start(FWD, 1)

    def piece(owner, i):
        if i < 4:
            return gu.at[owner, pl.ds(448 * i, 448), :]
        return dn.at[owner, pl.ds(128 * (i - 4), 128), :]

    for copy in weight_loads:
        copy.wait()
    to_mate = [remote(piece(seat, i), piece(seat, i), xs.at[i], xr.at[i], mate) for i in range(PIECES)]
    to_twin = [remote(piece(seat, i), piece(seat, i), cs.at[i], cr.at[i], twin) for i in range(PIECES)]
    passed = [
        remote(piece(mate_seat, i), piece(mate_seat, i), rs.at[i], rr.at[i], twin) for i in range(PIECES)
    ]
    for i in range(PIECES):
        to_mate[i].start()

    make_orders(1, bwd_routes)
    for a in (SAVED, COT):
        for copy in token_loads[a]:
            copy.wait()
        sort_rows(a, 1)
        gather_start(a, 1)

    expert = lax.broadcasted_iota(jnp.int32, (RING * PLANE, ROWS), 0)
    for m, (routes, mix) in enumerate(((fwd_routes, fwd_mix), (bwd_routes, bwd_mix))):
        spread = jnp.zeros((RING * PLANE, ROWS), jnp.float32)
        for k in range(TOP):
            spread = spread + jnp.where(routes[0, k : k + 1, :] == expert, mix[0, k : k + 1, :], 0.0)
        exact = dict(precision=lax.Precision.HIGHEST, preferred_element_type=jnp.float32)
        natural = jnp.dot(spread, order, **exact)
        for kind in range(4):
            if kind < 3:
                moved = perm[m, kind].astype(jnp.float32)
                value = lax.dot_general(natural, moved, (((1,), (1,)), ((), ())), **exact)
            else:
                value = natural
            for at in range(RING):
                wt[kind, at, pl.ds(4 * m, 4), :] = value[4 * at : 4 * at + 4, :]
        for way in (PLUS, MINUS):
            back[m, way] = perm[m, way].astype(jnp.float32).T.astype(jnp.bfloat16)

    def source_place(delta):
        if delta == 4:
            return FAR
        return place(delta, PLUS) if delta < 4 else place(RING - delta, MINUS)

    mixes = [
        remote(wt.at[(0 if d < 4 else 2 if d == 4 else 1), (y + d) % RING], wr.at[source_place(d)], ws.at[d - 1], wrs.at[d - 1], ring(d))
        for d in range(1, RING)
    ]
    for copy in mixes:
        copy.start()
    wr[OWN] = wt[3, y]

    @pl.when(core == 1)
    def _():
        pl.semaphore_wait(twin_here, 1)

    for i in range(PIECES):
        to_twin[i].start()

    relay(FWD, 1)
    relay(SAVED, 1)
    relay(COT, 1)
    for copy in mixes:
        copy.wait_recv()
    for s in range(RING):
        wc[pl.ds(s * ROWS, ROWS), :] = wr[s].T
    relay(FWD, 2)
    relay(SAVED, 2)
    relay(COT, 2)
    for i in range(PIECES):
        to_mate[i].wait_recv()
        passed[i].start()
    for i in range(PIECES):
        to_twin[i].wait_recv()
    for i in range(PIECES):
        passed[i].wait_recv()

    def compute_fwd(pair):
        rows = pl.ds(pair * 2 * ROWS, 2 * ROWS)
        for e in range(PLANE):
            projected = dot(x[FWD, rows, :], gu[e])
            gate, up = projected[:, :HID], projected[:, HID:]
            hidden = gate * jax.nn.sigmoid(gate) * up * wc[rows, e : e + 1]
            hid[:, e * HID : (e + 1) * HID] = hidden.astype(jnp.bfloat16)
        for n in range(WIDTH // 256):
            cols = slice(n * 256, (n + 1) * 256)
            total = dot(hid[:, :HID], dn[0, :, cols])
            for e in range(1, PLANE):
                total = total + dot(hid[:, e * HID : (e + 1) * HID], dn[e, :, cols])
            part[0, rows, cols] = total

    def compute_bwd(pair):
        rows = pl.ds(pair * 2 * ROWS, 2 * ROWS)
        for e in range(PLANE):
            projected = dot(x[SAVED, rows, :], gu[e])
            gate, up = projected[:, :HID], projected[:, HID:]
            d_hidden = dot_t(x[COT, rows, :], dn[e]) * wc[rows, 4 + e : 5 + e]
            sig = jax.nn.sigmoid(gate)
            d_gate = d_hidden * up * sig * (1.0 + gate * (1.0 - sig))
            d_up = d_hidden * gate * sig
            both[:, e * 2 * HID : e * 2 * HID + HID] = d_gate.astype(jnp.bfloat16)
            both[:, e * 2 * HID + HID : (e + 1) * 2 * HID] = d_up.astype(jnp.bfloat16)
        for n in range(WIDTH // 256):
            cols = slice(n * 256, (n + 1) * 256)
            total = dot_t(both[:, : 2 * HID], gu[0, cols, :])
            for e in range(1, PLANE):
                total = total + dot_t(both[:, e * 2 * HID : (e + 1) * 2 * HID], gu[e, cols, :])
            part[1, rows, cols] = total

    def back_copy(m, way, step, c):
        index = ((m * 2 + way) * 4 + step - 1) * 4 + c
        start, size = COLS[c]
        cols = pl.ds(start, size)
        count = BACK_ROWS[step]
        if step == 1:
            source = begun.at[m, way, :, cols]
        else:
            source = got.at[m, way, pl.ds(STEP_ROW[step - 1], count), cols]
        target = got.at[m, way, pl.ds(STEP_ROW[step], count), cols]
        return remote(source, target, ss.at[index], sr.at[index], side[1 - way])

    def back_begin(m):
        for c, (start, size) in enumerate(COLS):
            cols = slice(start, start + size)
            for way in (PLUS, MINUS):
                rows = pl.ds(FAR * ROWS + HOP_ROWS[4] * way, HOP_ROWS[4])
                begun[m, way, :, cols] = part[m, rows, cols].astype(jnp.bfloat16)
                back_copy(m, way, 1, c).start()

    def back_step(m, step):
        came, count = BACK_ROWS[step - 1], BACK_ROWS[step]
        for c, (start, size) in enumerate(COLS):
            cols = slice(start, start + size)
            for way in (PLUS, MINUS):
                block = place(5 - step, way) * ROWS
                back_copy(m, way, step - 1, c).wait_recv()
                rows = pl.ds(STEP_ROW[step - 1], came)
                total = got[m, way, rows, cols].astype(jnp.float32) + part[m, pl.ds(block, came), cols]
                got[m, way, rows, cols] = total.astype(jnp.bfloat16)
                if count > came:
                    rest = pl.ds(STEP_ROW[step - 1] + came, count - came)
                    mine = part[m, pl.ds(block + came, count - came), cols]
                    got[m, way, rest, cols] = mine.astype(jnp.bfloat16)
                back_copy(m, way, step, c).start()

    def out_copy(m, c, h):
        start, size = COLS[c]
        index = (m * 4 + c) * 4 + h
        return remote(
            done.at[m, pl.ds(PART * h, PART), pl.ds(start, size)],
            (out_fwd, out_bwd)[m].at[0, :, pl.ds(h * WIDTH + start, size)],
            os_.at[index], or_.at[index], (later, earlier)[m],
        )

    def finish(m):
        for c, (start, size) in enumerate(COLS):
            cols = slice(start, start + size)
            total = part[m, pl.ds(OWN * ROWS, ROWS), cols]
            for way in (PLUS, MINUS):
                back_copy(m, way, 4, c).wait_recv()
                total = total + dot(back[m, way], got[m, way, pl.ds(STEP_ROW[4], ROWS), cols])
            done[m, :, cols] = total.astype(jnp.bfloat16)
            for h in range(4):
                out_copy(m, c, h).start()

    compute_fwd(1)
    relay(FWD, 3)
    compute_fwd(2)
    relay(SAVED, 3)
    compute_fwd(3)
    compute_bwd(1)
    relay(COT, 3)
    gather_wait(FWD, 4)
    compute_fwd(0)
    back_begin(0)
    compute_bwd(2)
    back_step(0, 2)
    compute_bwd(3)
    back_step(0, 3)
    gather_wait(SAVED, 4)
    gather_wait(COT, 4)
    compute_bwd(0)
    back_begin(1)
    back_step(0, 4)
    back_step(1, 2)

    @pl.when(odd == 0)
    def _():
        pl.semaphore_wait(pipe_here, 2)

    finish(0)
    back_step(1, 3)
    back_step(1, 4)
    finish(1)

    for a in (FWD, SAVED, COT):
        for hop in range(1, 5):
            for way in (PLUS, MINUS):
                gather(a, way, hop).wait_send()
    for i in range(PIECES):
        to_mate[i].wait_send()
        to_twin[i].wait_send()
        passed[i].wait_send()
    for copy in mixes:
        copy.wait_send()
    for m in range(2):
        for c in range(4):
            for step in range(1, 5):
                for way in (PLUS, MINUS):
                    back_copy(m, way, step, c).wait_send()
            for h in range(4):
                out_copy(m, c, h).wait_send()
                out_copy(m, c, h).wait_recv()


def deliver(fwd, bwd, out_fwd, out_bwd):
    out_fwd[...] = fwd[...]
    out_bwd[...] = bwd[...]


def body(fwd_tokens, fwd_routes, fwd_mix, saved, cotangent, bwd_routes, bwd_mix, gate_up, down):
    fwd_routes, fwd_mix, bwd_routes, bwd_mix = (
        jnp.swapaxes(v, 1, 2) for v in (fwd_routes, fwd_mix, bwd_routes, bwd_mix)
    )
    operands = (
        fwd_tokens, fwd_routes, fwd_mix, saved, cotangent, bwd_routes, bwd_mix, gate_up, down
    )
    hbm = pl.BlockSpec(memory_space=pl.ANY)
    vmem = pl.BlockSpec(memory_space=pltpu.VMEM)
    out = jax.ShapeDtypeStruct(operands[0].shape, jnp.bfloat16)
    dma = pltpu.SemaphoreType.DMA
    bf16, f32 = jnp.bfloat16, jnp.float32
    moved = pl.pallas_call(
        kernel,
        out_shape=(out, out),
        in_specs=[hbm, vmem, vmem, hbm, hbm, vmem, vmem, hbm, hbm],
        out_specs=(hbm, hbm),
        scratch_shapes=[
            pltpu.VMEM((3, RING * ROWS, WIDTH), bf16),
            pltpu.VMEM((3, 2, ROWS, WIDTH), bf16),
            pltpu.VMEM((PLANE, WIDTH, 2 * HID), bf16),
            pltpu.VMEM((PLANE, HID, WIDTH), bf16),
            pltpu.VMEM((2, RING * ROWS, WIDTH), f32),
            pltpu.VMEM((2, 2, GOT_ROWS, WIDTH), bf16),
            pltpu.VMEM((2, 2, HOP_ROWS[4], WIDTH), bf16),
            pltpu.VMEM((2, ROWS, WIDTH), bf16),
            pltpu.VMEM((2 * ROWS, PLANE * HID), bf16),
            pltpu.VMEM((2 * ROWS, PLANE * 2 * HID), bf16),
            pltpu.VMEM((2, 3, ROWS, ROWS), bf16),
            pltpu.VMEM((2, 2, ROWS, ROWS), bf16),
            pltpu.VMEM((4, RING, 8, ROWS), f32),
            pltpu.VMEM((RING, 8, ROWS), f32),
            pltpu.VMEM((RING * ROWS, 8), f32),
            dma((14,)),
            dma((24,)), dma((24,)),
            dma((64,)), dma((64,)),
            dma((32,)), dma((32,)),
            dma((PIECES,)), dma((PIECES,)),
            dma((PIECES,)), dma((PIECES,)),
            dma((PIECES,)), dma((PIECES,)),
            dma((RING - 1,)), dma((RING - 1,)),
            pltpu.SemaphoreType.REGULAR,
            pltpu.SemaphoreType.REGULAR,
        ],
        name="moe_relay",
        compiler_params=pltpu.CompilerParams(
            collective_id=0, has_side_effects=True, vmem_limit_bytes=60 * 1024 * 1024
        ),
    )(*operands)
    return pl.pallas_call(
        deliver,
        out_shape=(out, out),
        in_specs=[vmem, vmem],
        out_specs=(vmem, vmem),
        name="deliver",
    )(*moved)


def solution(mesh):
    spec3 = P("pipe", "expert", None)
    spec4 = P("pipe", "expert", None, None)
    return jax.shard_map(
        body,
        mesh=mesh,
        in_specs=(spec3,) * 7 + (spec4,) * 2,
        out_specs=(spec3, spec3),
        check_vma=False,
    )
```
